32 devices in a mesh: row: 4 (over y, x), col: 8 (over z, core).
Axes of the slice: x: 2, y: 2, z: 4, core: 2. Of those that a mesh axis runs over, the one named last changes fastest.
Arguments:
- trail: bfloat16 [1024, 24576], P('row', 'col'), may hold values from -6 to 6
- trail_rows: int32 [16, 192], P('row', 'col'), may hold values from 0 to 47, as said below
- owner_x: bfloat16 [16384, 1024], P(('row', 'col')), may hold values from -0.1875 to 0.1875
- owner_y: bfloat16 [16384, 1024], P(('row', 'col')), may hold values from -6 to 6
- owner_of: int32 [192], replicated, may hold values from 0 to 7, as said below
- inv_first: bfloat16 [2, 256, 256], replicated, may hold values from -0.25 to 0.25
- inv_second: bfloat16 [2, 256, 256], replicated, may hold values from -0.25 to 0.25
- couple_right: bfloat16 [2, 256, 256], replicated, may hold values from -0.25 to 0.25
- couple_left: bfloat16 [2, 256, 256], replicated, may hold values from -0.25 to 0.25
Outputs:
- updated_trail: bfloat16 [1024, 24576], P('row', 'col')
The draws below stay inside these ranges and needn't reach their ends.
Inputs may be any that keep to these rules, and one draw needn't show every extreme that they name: `trail_rows`: for each grid row and each block column, the 4 entries in rows r * 4 to r * 4 + 3 are distinct local block rows. `owner_of`: the 6 blocks r * 48 + c * 6 + k (k < 6) have distinct owners; one owner holds at most 8 blocks of its grid row, and some owner of every grid row holds exactly 8.
All inputs are finite; a program needn't handle non-finite values.
Results may differ from the reference program's by a relative error of at most 0.0062.
Values may be sent and summed in bfloat16 or wider, within the bound.
A program may use at most 128 MiB of HBM per device.

```python
import jax
import jax.numpy as jnp
from jax import lax

BS = 64
PANEL = 256
PER = 6
GRID_ROWS = 4
GRID_COLS = 8
CAP = 8
NBR = 48
NBC = 24
FILLK = 4
BLOCKS = 192
TRAIL = 12288


def draw_trail_rows(key, part):
    scores = jax.random.randint(jax.random.fold_in(key, 7), (GRID_ROWS, BLOCKS, NBR), 0, 1 << 20, dtype=jnp.int32)
    scores = scores * NBR + jnp.arange(NBR, dtype=jnp.int32)[None, None, :]
    chosen = lax.top_k(scores, FILLK)[1].astype(jnp.int32)
    return jnp.transpose(chosen, (0, 2, 1)).reshape(GRID_ROWS * FILLK, BLOCKS)


def permute_owners(single_key):
    return jax.random.permutation(single_key, GRID_COLS).astype(jnp.int32)


def draw_owner_of(key, part):
    key_perm = jax.random.fold_in(key, 11)
    key_order = jax.random.fold_in(key, 23)
    owner_perm = jax.vmap(permute_owners)(jax.random.split(key_perm, GRID_ROWS))
    spare_count = GRID_COLS - 2
    extra_count = PER - 2
    dest_index = jnp.arange(GRID_COLS, dtype=jnp.int32)[:, None]
    position = jnp.arange(PER, dtype=jnp.int32)[None, :]
    rank_table = jnp.where(position < 2, position, 2 + (dest_index * extra_count + position - 2) % spare_count)
    scores = jax.random.randint(key_order, (GRID_ROWS, GRID_COLS, PER), 0, 1 << 20, dtype=jnp.int32)
    scores = scores * PER + position[None, :, :]
    shuffle_order = jnp.argsort(scores, axis=-1, stable=True)
    rank_full = jnp.broadcast_to(rank_table[None, :, :], (GRID_ROWS, GRID_COLS, PER))
    shuffled = jnp.take_along_axis(rank_full, shuffle_order, axis=-1)
    owners = jnp.take_along_axis(owner_perm, shuffled.reshape(GRID_ROWS, GRID_COLS * PER), axis=1)
    return owners.reshape(BLOCKS).astype(jnp.int32)


def block_scale(rng, dims, shards, low, largest):
    level = 1.0
    for axis_at, blocks in shards:
        draws = jax.random.uniform(jax.random.fold_in(jax.random.fold_in(rng, 6), axis_at), (blocks,), jnp.float32, low / len(shards), largest / len(shards))
        level = level * jnp.repeat(jnp.exp(draws), dims[axis_at] // blocks).reshape((-1,) + (1,) * (len(dims) - 1 - axis_at))
    return level


def gaussian(own_key, extent, width, bound, shards=(), kind=jnp.bfloat16):
    array = jax.random.normal(own_key, extent, jnp.float32) * width
    if len(shards) > 0:
        array = block_scale(own_key, extent, shards, -0.22, 0.18) * array
    return jnp.clip(array, min=-bound, max=bound).astype(kind)


def setup_inputs(seed: int = 0) -> dict:
    key_list = jax.random.split(jax.random.key(seed), 10)
    trail = gaussian(key_list[0], (GRID_ROWS * FILLK * BS, 2 * TRAIL), 1.0, 6.0, ((0, 4), (1, 8)))
    trail_rows = draw_trail_rows(jax.random.fold_in(key_list[9], 71), 0)
    owner_x = gaussian(key_list[2], (GRID_ROWS * GRID_COLS * CAP * BS, 4 * PANEL), 0.03125, 0.1875, ((0, 32),))
    owner_y = gaussian(key_list[3], (GRID_ROWS * GRID_COLS * CAP * BS, 4 * PANEL), 1.0, 6.0, ((0, 32),))
    owner_of = draw_owner_of(jax.random.fold_in(key_list[9], 71), 0)
    inv_first = gaussian(key_list[5], (2, PANEL, PANEL), (2 * PANEL) ** -0.5, 0.25)
    inv_second = gaussian(key_list[6], (2, PANEL, PANEL), (2 * PANEL) ** -0.5, 0.25)
    couple_right = gaussian(key_list[7], (2, PANEL, PANEL), (2 * PANEL) ** -0.5, 0.25)
    couple_left = gaussian(key_list[8], (2, PANEL, PANEL), (2 * PANEL) ** -0.5, 0.25)
    return {"trail": trail, "trail_rows": trail_rows, "owner_x": owner_x, "owner_y": owner_y, "owner_of": owner_of, "inv_first": inv_first, "inv_second": inv_second, "couple_right": couple_right, "couple_left": couple_left}


def real_form(pair):
    top_rows = jnp.concatenate([pair[0], pair[1]], axis=1)
    low_rows = jnp.concatenate([-pair[1], pair[0]], axis=1)
    return jnp.concatenate([top_rows, low_rows], axis=0)


def halves(matrix):
    first_half = jnp.concatenate([matrix[:, :PANEL], matrix[:, 2 * PANEL:3 * PANEL]], axis=1)
    second_half = jnp.concatenate([matrix[:, PANEL:2 * PANEL], matrix[:, 3 * PANEL:]], axis=1)
    return first_half, second_half


def join_panels(left_part, right_part):
    return jnp.concatenate([left_part[:, :PANEL], right_part[:, :PANEL], left_part[:, PANEL:], right_part[:, PANEL:]], axis=1)


def form_rows(matrix, inv_first, inv_second, couple_right):
    first_half, second_half = halves(matrix)
    low_first = jnp.dot(first_half, real_form(inv_first), preferred_element_type=jnp.float32).astype(jnp.bfloat16)
    remainder = second_half.astype(jnp.float32) - jnp.dot(low_first, real_form(couple_right), preferred_element_type=jnp.float32)
    remainder = remainder.astype(jnp.bfloat16)
    low_second = jnp.dot(remainder, real_form(inv_second), preferred_element_type=jnp.float32).astype(jnp.bfloat16)
    return join_panels(low_first, low_second)


def form_cols(matrix, inv_first, couple_left):
    coupling = jnp.dot(jnp.concatenate([couple_left[0], couple_left[1]], axis=1), real_form(inv_first), preferred_element_type=jnp.float32).astype(jnp.bfloat16)
    transposed = jnp.stack([coupling[:, :PANEL].T, coupling[:, PANEL:].T])
    first_half, second_half = halves(matrix)
    remainder = second_half.astype(jnp.float32) - jnp.dot(first_half, real_form(transposed), preferred_element_type=jnp.float32)
    return join_panels(first_half, remainder.astype(jnp.bfloat16))


def stack_cols(upper_rows):
    count = upper_rows.shape[0] // BS
    real_part = upper_rows[:, :2 * PANEL]
    imag_part = upper_rows[:, 2 * PANEL:]
    top_rows = jnp.concatenate([real_part, -imag_part], axis=1).reshape(count, BS, 4 * PANEL)
    low_rows = jnp.concatenate([imag_part, real_part], axis=1).reshape(count, BS, 4 * PANEL)
    return jnp.concatenate([top_rows, low_rows], axis=1)


def reference(trail, trail_rows, owner_x, owner_y, owner_of, inv_first, inv_second, couple_right, couple_left):
    owners = owner_of.reshape(GRID_ROWS, NBR)
    owner_marks = (owners[:, :, None] == jnp.arange(GRID_COLS, dtype=jnp.int32)[None, None, :]).astype(jnp.int32)
    before = jnp.cumsum(owner_marks, axis=1, dtype=jnp.int32) - owner_marks
    slot_index = jnp.sum(before * owner_marks, axis=2, dtype=jnp.int32)
    source = (jnp.arange(GRID_ROWS, dtype=jnp.int32)[:, None] * GRID_COLS + owners) * CAP + slot_index
    source = source.reshape(BLOCKS).astype(jnp.int32)
    x_blocks = owner_x.reshape(GRID_ROWS * GRID_COLS * CAP, BS, 4 * PANEL)[source].reshape(TRAIL, 4 * PANEL)
    y_blocks = owner_y.reshape(GRID_ROWS * GRID_COLS * CAP, BS, 4 * PANEL)[source].reshape(TRAIL, 4 * PANEL)
    lower_rows = form_rows(x_blocks, inv_first, inv_second, couple_right).reshape(GRID_ROWS, NBR, BS, 4 * PANEL)
    upper_rows = form_cols(y_blocks, inv_first, couple_left)
    stacked = stack_cols(upper_rows).reshape(GRID_ROWS, GRID_COLS, PER, 2 * BS, 4 * PANEL)
    stacked = jnp.transpose(stacked, (1, 0, 2, 3, 4)).reshape(GRID_COLS, NBC, 2 * BS, 4 * PANEL).astype(jnp.float32)
    trail_tiles = trail.reshape(GRID_ROWS * FILLK, BS, GRID_COLS, NBC, 2 * BS)
    pattern = trail_rows.reshape(GRID_ROWS * FILLK, GRID_COLS, NBC)
    grid_groups = jnp.arange(GRID_ROWS * FILLK, dtype=jnp.int32) // FILLK

    def one_group(inputs):
        block_tile, pattern_rows, grid_row = inputs
        rows_here = lax.dynamic_index_in_dim(lower_rows, grid_row, 0, keepdims=False)
        picked = rows_here[pattern_rows].astype(jnp.float32)
        change = jnp.einsum('cjbp,cjqp->bcjq', picked, stacked)
        return (block_tile.astype(jnp.float32) - change).astype(jnp.bfloat16)

    updated = lax.map(one_group, (trail_tiles, pattern, grid_groups))
    return updated.reshape(GRID_ROWS * FILLK * BS, 2 * TRAIL)
```

```python
import functools

import jax
import jax.numpy as jnp
from jax import lax
from jax.experimental import pallas as pl
from jax.experimental.pallas import tpu as pltpu
from jax.sharding import PartitionSpec as P

BS = 64
PANEL = 256
PER = 6
PARTS = 4
CH = 2 * PANEL // PARTS
MESH = pl.DeviceIdType.MESH
F32 = jnp.float32
BF16 = jnp.bfloat16


def dot_t(a, b):
    return lax.dot_general(a, b, (((1,), (1,)), ((), ())), preferred_element_type=F32)


def half(block, at):
    lo = at * PANEL
    return jnp.concatenate(
        [block[:, lo : lo + PANEL], block[:, 2 * PANEL + lo : 3 * PANEL + lo]], axis=1
    )


def stacked(w_real, w_imag):
    return jnp.concatenate(
        [
            jnp.concatenate([w_real, -w_imag], axis=1),
            jnp.concatenate([w_imag, w_real], axis=1),
        ],
        axis=0,
    )


def w_part(w_half, p):
    at = (p % 2) * CH
    return stacked(w_half[:, at : at + CH], w_half[:, PANEL + at : PANEL + at + CH])


def body(sizes, *refs):
    rows, cols, cap, fill, width, fused = sizes
    slots_ref, lidx_ref, widx_ref, x_ref, y_ref, inv1, inv2, cr, cl = refs[:9]
    refs = refs[9:]
    if fused:
        trail_ref, out_ref = refs[:2]
        refs = refs[2:]
    l_all, w_all = refs[:PARTS], refs[PARTS : PARTS + 2]
    refs = refs[PARTS + 2 :]
    if fused:
        acc, trail_v, trail_sem = refs[:3]
        refs = refs[3:]
    own_l, stage, w_low, rf, gt, ysend, yrecv, wsend, wrecv, lsend, lrecv, lcopy, ycopy = refs
    row = lax.axis_index("row")
    col = lax.axis_index("col")
    chips = cols // 2
    z = col // 2
    core = col % 2
    tile = 4
    n_tiles = cap // tile

    if fused:
        trail_copy = pltpu.make_async_copy(trail_ref, trail_v, trail_sem)
        trail_copy.start()

    barrier = pltpu.get_barrier_semaphore()
    for d in range(1, cols):
        pl.semaphore_signal(
            barrier, inc=1, device_id=(row, lax.rem(col + d, cols)), device_id_type=MESH
        )
    for d in range(1, rows):
        pl.semaphore_signal(
            barrier, inc=1, device_id=(lax.rem(row + d, rows), col), device_id_type=MESH
        )

    for c in range(cols):
        stage[0, c] = half(y_ref[slots_ref[c]], 0)

    pl.semaphore_wait(barrier, cols + rows - 2)

    def send_y(h):
        for d in range(1, cols):
            to = lax.rem(col + d, cols)
            pltpu.make_async_remote_copy(
                src_ref=stage.at[h, to],
                dst_ref=w_all[h].at[row * cols + col],
                send_sem=ysend.at[h, to],
                recv_sem=yrecv.at[h, col],
                device_id=(row, to),
                device_id_type=MESH,
            ).start()
        pltpu.make_async_copy(
            stage.at[h, col], w_all[h].at[row * cols + col], ycopy.at[h]
        ).start()

    def y_copy(h, o):
        return pltpu.make_async_remote_copy(
            src_ref=stage.at[h, o],
            dst_ref=w_all[h].at[row * cols + o],
            send_sem=ysend.at[h, o],
            recv_sem=yrecv.at[h, o],
            device_id=(row, o),
            device_id_type=MESH,
        )

    def w_copy(h, r, to):
        return pltpu.make_async_remote_copy(
            src_ref=w_all[h].at[pl.ds(r * cols, cols)],
            dst_ref=w_all[h].at[pl.ds(r * cols, cols)],
            send_sem=wsend.at[h, to],
            recv_sem=wrecv.at[h, r],
            device_id=(to, col),
            device_id_type=MESH,
        )

    def spread_w(h):
        for d in range(1, cols):
            y_copy(h, lax.rem(col + d, cols)).wait_recv()
        pltpu.make_async_copy(
            stage.at[h, col], w_all[h].at[row * cols + col], ycopy.at[h]
        ).wait()
        for d in range(1, rows):
            w_copy(h, row, lax.rem(row + d, rows)).start()

    def await_w(h):
        for d in range(1, rows):
            r = lax.rem(row + d, rows)
            w_copy(h, r, r).wait_recv()

    def l_copy(p, o, way, own):
        place = l_all[p].at[pl.ds(o * cap, cap)]
        to = (col - 2, col + 2, col + 1 - 2 * core)[way]
        return pltpu.make_async_remote_copy(
            src_ref=own_l.at[p] if own else place,
            dst_ref=place,
            send_sem=lsend.at[p, o, way],
            recv_sem=lrecv.at[p, o],
            device_id=(row, to),
            device_id_type=MESH,
        )

    def l_own(p):
        return pltpu.make_async_copy(
            own_l.at[p], l_all[p].at[pl.ds(col * cap, cap)], lcopy.at[p]
        )

    def send_own(p):
        @pl.when(z > 0)
        def _():
            l_copy(p, col, 0, True).start()

        @pl.when(z < chips - 1)
        def _():
            l_copy(p, col, 1, True).start()

        l_copy(p, col, 2, True).start()
        l_own(p).start()

    def relay(p):
        for d in range(1, chips):
            left = col - 2 * d
            right = col + 2 * d

            @pl.when(z >= d)
            def _():
                l_copy(p, left, 1, False).wait_recv()

                @pl.when(z < chips - 1)
                def _():
                    l_copy(p, left, 1, False).start()

                l_copy(p, left, 2, False).start()

            @pl.when(z + d < chips)
            def _():
                l_copy(p, right, 0, False).wait_recv()

                @pl.when(z > 0)
                def _():
                    l_copy(p, right, 0, False).start()

                l_copy(p, right, 2, False).start()

    def await_l(p):
        l_own(p).wait()
        for chip in range(chips):
            l_copy(p, 2 * chip + 1 - core, 2, False).wait_recv()

    def l_drain(p):
        @pl.when(z > 0)
        def _():
            l_copy(p, col, 0, True).wait_send()

        @pl.when(z < chips - 1)
        def _():
            l_copy(p, col, 1, True).wait_send()

        l_copy(p, col, 2, True).wait_send()
        for d in range(1, chips):
            left = col - 2 * d
            right = col + 2 * d

            @pl.when(z >= d)
            def _():
                @pl.when(z < chips - 1)
                def _():
                    l_copy(p, left, 1, False).wait_send()

                l_copy(p, left, 2, False).wait_send()

            @pl.when(z + d < chips)
            def _():
                @pl.when(z > 0)
                def _():
                    l_copy(p, right, 0, False).wait_send()

                l_copy(p, right, 2, False).wait_send()

    def set_real_form(at, pair):
        rf[at, :PANEL, :PANEL] = pair[0]
        rf[at, :PANEL, PANEL:] = pair[1]
        rf[at, PANEL:, :PANEL] = -pair[1]
        rf[at, PANEL:, PANEL:] = pair[0]

    send_y(0)

    set_real_form(0, inv1)
    coupling = jnp.dot(
        jnp.concatenate([cl[0], cl[1]], axis=1), rf[0], preferred_element_type=F32
    ).astype(BF16)
    gt[:PANEL, :PANEL] = coupling[:, :PANEL]
    gt[:PANEL, PANEL:] = -coupling[:, PANEL:]
    gt[PANEL:, :PANEL] = coupling[:, PANEL:]
    gt[PANEL:, PANEL:] = coupling[:, :PANEL]

    def low_w(i, carry):
        block = y_ref[pl.ds(i * tile, tile)].reshape(tile * BS, 4 * PANEL)
        low = half(block, 1).astype(F32) - dot_t(half(block, 0), gt[...])
        w_low[pl.ds(i * tile, tile)] = low.astype(BF16).reshape(tile, BS, 2 * PANEL)
        return carry

    lax.fori_loop(0, n_tiles, low_w, 0)
    for c in range(cols):
        stage[1, c] = w_low[slots_ref[c]]
    send_y(1)

    def put_l(i, first, value):
        for k in range(2):
            part = jnp.concatenate(
                [
                    value[:, k * CH : (k + 1) * CH],
                    value[:, PANEL + k * CH : PANEL + (k + 1) * CH],
                ],
                axis=1,
            )
            own_l[first + k, pl.ds(i * tile, tile)] = part.reshape(tile, BS, 2 * CH)

    def first_l(i, carry):
        block = x_ref[pl.ds(i * tile, tile)].reshape(tile * BS, 4 * PANEL)
        value = jnp.dot(half(block, 0), rf[0], preferred_element_type=F32).astype(BF16)
        put_l(i, 0, value)
        return carry

    lax.fori_loop(0, n_tiles, first_l, 0)
    send_own(0)

    set_real_form(1, cr)
    set_real_form(2, inv2)

    def second_l(i, carry):
        block = x_ref[pl.ds(i * tile, tile)].reshape(tile * BS, 4 * PANEL)
        parts = [
            own_l[k, pl.ds(i * tile, tile)].reshape(tile * BS, 2 * CH) for k in range(2)
        ]
        low = jnp.concatenate(
            [parts[0][:, :CH], parts[1][:, :CH], parts[0][:, CH:], parts[1][:, CH:]], axis=1
        )
        rest = half(block, 1).astype(F32) - jnp.dot(low, rf[1], preferred_element_type=F32)
        value = jnp.dot(rest.astype(BF16), rf[2], preferred_element_type=F32).astype(BF16)
        put_l(i, 2, value)
        return carry

    lax.fori_loop(0, n_tiles, second_l, 0)

    def update(p):
        h = p // 2

        def column(q, carry):
            rhs = w_part(w_all[h][widx_ref[q]], p)
            lhs = jnp.concatenate(
                [l_all[p][lidx_ref[s * width + q]] for s in range(fill)], axis=0
            )
            change = dot_t(lhs, rhs)
            lanes = pl.ds(pl.multiple_of(q * 2 * BS, 2 * BS), 2 * BS)
            if p == 0:
                acc[q] = trail_v[:, lanes].astype(F32) - change
            elif p < PARTS - 1:
                acc[q] = acc[q] - change
            else:
                out_ref[:, lanes] = (acc[q] - change).astype(BF16)
            return carry

        lax.fori_loop(0, width, column, 0)

    def finish(p):
        await_l(p)
        if p % 2 == 0:
            await_w(p // 2)
        if fused:
            if p == 0:
                trail_copy.wait()
            update(p)

    spread_w(0)
    relay(0)
    spread_w(1)
    for p in range(1, PARTS):
        send_own(p)
        finish(p - 1)
        relay(p)
    finish(PARTS - 1)

    for h in range(2):
        for d in range(1, cols):
            y_copy(h, lax.rem(col + d, cols)).wait_send()
        for d in range(1, rows):
            w_copy(h, row, lax.rem(row + d, rows)).wait_send()
    for p in range(PARTS):
        l_drain(p)


def pick_body(lidx_ref, widx_ref, *refs):
    l_refs, w_refs = refs[:PARTS], refs[PARTS : PARTS + 2]
    trail_ref, out_ref = refs[PARTS + 2 :]
    total = trail_ref[...].astype(F32)
    for p in range(PARTS):
        total = total - dot_t(l_refs[p][0], w_part(w_refs[p // 2][0], p))
    out_ref[...] = total.astype(BF16)


def plan(trail_rows, owner_of, rows, cols, cap):
    my_row = lax.axis_index("row")
    my_col = lax.axis_index("col")
    count = PER * cols
    grid = owner_of.reshape(rows, count)
    owners = lax.dynamic_index_in_dim(grid, my_row, 0, keepdims=False)
    at = jnp.arange(count, dtype=jnp.int32)
    same = (owners[:, None] == owners[None, :]) & (at[None, :] < at[:, None])
    slot = jnp.sum(same.astype(jnp.int32), axis=1, dtype=jnp.int32)
    place = owners * cap + slot
    lidx = jnp.sum(
        jnp.where(trail_rows[:, :, None] == at, place, 0), axis=2, dtype=jnp.int32
    )
    slots = jnp.sum(
        jnp.where(owners == my_col, slot, 0).reshape(cols, PER), axis=1, dtype=jnp.int32
    )
    wanted = lax.dynamic_index_in_dim(
        owner_of.reshape(rows, cols, PER), my_col, 1, keepdims=False
    )
    widx = wanted + cols * jnp.arange(rows, dtype=jnp.int32)[:, None]
    return slots, lidx.reshape(-1), widx.reshape(-1)


def local(mesh, trail, trail_rows, owner_x, owner_y, owner_of, inv1, inv2, cr, cl):
    rows, cols = mesh.shape["row"], mesh.shape["col"]
    cap = owner_x.shape[0] // BS
    fill = trail.shape[0] // BS
    width = trail.shape[1] // (2 * BS)
    l_shape = (cols * cap, BS, 2 * CH)
    w_shape = (rows * cols, BS, 2 * PANEL)
    fused = cols * cap * BS * 4 * PANEL * 2 <= 16 << 20
    slots, lidx, widx = plan(trail_rows, owner_of, rows, cols, cap)
    blocks = (cap, BS, 4 * PANEL)
    operands = [
        slots, lidx, widx, owner_x.reshape(blocks), owner_y.reshape(blocks), inv1, inv2, cr, cl,
    ]
    smem = pl.BlockSpec(memory_space=pltpu.SMEM)
    vmem = pl.BlockSpec(memory_space=pltpu.VMEM)
    anywhere = pl.BlockSpec(memory_space=pl.ANY)
    in_specs = [smem] * 3 + [vmem] * 6
    scratch = [
        pltpu.VMEM((PARTS, cap, BS, 2 * CH), BF16),
        pltpu.VMEM((2, cols, BS, 2 * PANEL), BF16),
        pltpu.VMEM((cap, BS, 2 * PANEL), BF16),
        pltpu.VMEM((3, 2 * PANEL, 2 * PANEL), BF16),
        pltpu.VMEM((2 * PANEL, 2 * PANEL), BF16),
        pltpu.SemaphoreType.DMA((2, cols)),
        pltpu.SemaphoreType.DMA((2, cols)),
        pltpu.SemaphoreType.DMA((2, rows)),
        pltpu.SemaphoreType.DMA((2, rows)),
        pltpu.SemaphoreType.DMA((PARTS, cols, 3)),
        pltpu.SemaphoreType.DMA((PARTS, cols)),
        pltpu.SemaphoreType.DMA((PARTS,)),
        pltpu.SemaphoreType.DMA((2,)),
    ]
    if fused:
        operands.append(trail)
        in_specs.append(anywhere)
        out_shape = jax.ShapeDtypeStruct(trail.shape, BF16)
        out_specs = vmem
        scratch = [pltpu.VMEM(l_shape, BF16)] * PARTS + [pltpu.VMEM(w_shape, BF16)] * 2 + [
            pltpu.VMEM((width, fill * BS, 2 * BS), F32),
            pltpu.VMEM(trail.shape, BF16),
            pltpu.SemaphoreType.DMA,
        ] + scratch
    else:
        out_shape = [jax.ShapeDtypeStruct(l_shape, BF16)] * PARTS
        out_shape += [jax.ShapeDtypeStruct(w_shape, BF16)] * 2
        out_specs = [anywhere] * (PARTS + 2)
    result = pl.pallas_call(
        functools.partial(body, (rows, cols, cap, fill, width, fused)),
        out_shape=out_shape,
        in_specs=in_specs,
        out_specs=out_specs,
        scratch_shapes=scratch,
        compiler_params=pltpu.CompilerParams(
            collective_id=0, has_side_effects=True, vmem_limit_bytes=48 << 20
        ),
    )(*operands)
    if fused:
        return result
    return pl.pallas_call(
        pick_body,
        out_shape=jax.ShapeDtypeStruct(trail.shape, BF16),
        grid_spec=pltpu.PrefetchScalarGridSpec(
            num_scalar_prefetch=2,
            grid=(width, fill),
            in_specs=[
                pl.BlockSpec((1, BS, 2 * CH), lambda q, s, li, wi: (li[s * width + q], 0, 0))
            ]
            * PARTS
            + [pl.BlockSpec((1, BS, 2 * PANEL), lambda q, s, li, wi: (wi[q], 0, 0))] * 2
            + [pl.BlockSpec((BS, 2 * BS), lambda q, s, li, wi: (s, q))],
            out_specs=pl.BlockSpec((BS, 2 * BS), lambda q, s, li, wi: (s, q)),
        ),
    )(lidx, widx, *result, trail)


def solution(mesh):
    both = P(("row", "col"), None)
    placed = (P("row", "col"), P("row", "col"), both, both, P(), P(), P(), P(), P())
    return jax.shard_map(
        functools.partial(local, mesh),
        mesh=mesh,
        in_specs=placed,
        out_specs=P("row", "col"),
        check_vma=False,
    )
```

```python
import functools

import jax
import jax.numpy as jnp
from jax import lax
from jax.experimental import pallas as pl
from jax.experimental.pallas import tpu as pltpu
from jax.sharding import PartitionSpec as P

BS = 64
PANEL = 256
PER = 6
PARTS = 4
CH = 2 * PANEL // PARTS
MESH = pl.DeviceIdType.MESH
F32 = jnp.float32
BF16 = jnp.bfloat16


def dot_t(a, b):
    return lax.dot_general(a, b, (((1,), (1,)), ((), ())), preferred_element_type=F32)


def half(block, at):
    lo = at * PANEL
    return jnp.concatenate(
        [block[:, lo : lo + PANEL], block[:, 2 * PANEL + lo : 3 * PANEL + lo]], axis=1
    )


def stacked(w_real, w_imag):
    return jnp.concatenate(
        [
            jnp.concatenate([w_real, -w_imag], axis=1),
            jnp.concatenate([w_imag, w_real], axis=1),
        ],
        axis=0,
    )


def w_part(w_half, p):
    at = (p % 2) * CH
    return stacked(w_half[:, at : at + CH], w_half[:, PANEL + at : PANEL + at + CH])


def body(sizes, *refs):
    rows, cols, cap, fill, width, fused = sizes
    place_ref, owner_ref, picks_ref = refs[:3]
    sources = refs[3:9]
    refs = refs[9:]
    if fused:
        trail_ref, out_ref = refs[:2]
        refs = refs[2:]
    l_all, w_all = refs[:PARTS], refs[PARTS : PARTS + 2]
    refs = refs[PARTS + 2 :]
    if fused:
        acc, trail_v, trail_sem = refs[:3]
        refs = refs[3:]
    own_l, stage, w_low, rf, gt = refs[:5]
    held = refs[5:11]
    y_ref, cl, inv1, x_ref, cr, inv2 = held
    fetched, ysend, yrecv, wsend, wrecv, lsend, lrecv, lcopy, ycopy = refs[11:]
    row = lax.axis_index("row")
    col = lax.axis_index("col")
    chips = cols // 2
    z = col // 2
    core = col % 2
    tile = 4
    n_tiles = cap // tile

    fetch = [
        pltpu.make_async_copy(sources[i], held[i], fetched.at[i]) for i in range(len(held))
    ]
    for copy in fetch:
        copy.start()
    if fused:
        trail_copy = pltpu.make_async_copy(trail_ref, trail_v, trail_sem)
        trail_copy.start()

    barrier = pltpu.get_barrier_semaphore()
    for d in range(1, cols):
        pl.semaphore_signal(
            barrier, inc=1, device_id=(row, lax.rem(col + d, cols)), device_id_type=MESH
        )
    for d in range(1, rows):
        pl.semaphore_signal(
            barrier, inc=1, device_id=(lax.rem(row + d, rows), col), device_id_type=MESH
        )

    slots = []
    for c in range(cols):
        slot = 0
        for k in range(c * PER, (c + 1) * PER):
            mine = owner_ref[row * (PER * cols) + k] == col
            slot = slot + jnp.where(mine, place_ref[k] - col * cap, 0)
        slots.append(slot)

    fetch[0].wait()
    for c in range(cols):
        stage[0, c] = half(y_ref[slots[c]], 0)

    pl.semaphore_wait(barrier, cols + rows - 2)

    def send_y(h):
        for d in range(1, cols):
            to = lax.rem(col + d, cols)
            pltpu.make_async_remote_copy(
                src_ref=stage.at[h, to],
                dst_ref=w_all[h].at[row * cols + col],
                send_sem=ysend.at[h, to],
                recv_sem=yrecv.at[h, col],
                device_id=(row, to),
                device_id_type=MESH,
            ).start()
        pltpu.make_async_copy(
            stage.at[h, col], w_all[h].at[row * cols + col], ycopy.at[h]
        ).start()

    def y_copy(h, o):
        return pltpu.make_async_remote_copy(
            src_ref=stage.at[h, o],
            dst_ref=w_all[h].at[row * cols + o],
            send_sem=ysend.at[h, o],
            recv_sem=yrecv.at[h, o],
            device_id=(row, o),
            device_id_type=MESH,
        )

    def w_copy(h, r, to):
        return pltpu.make_async_remote_copy(
            src_ref=w_all[h].at[pl.ds(r * cols, cols)],
            dst_ref=w_all[h].at[pl.ds(r * cols, cols)],
            send_sem=wsend.at[h, to],
            recv_sem=wrecv.at[h, r],
            device_id=(to, col),
            device_id_type=MESH,
        )

    def spread_w(h):
        for d in range(1, cols):
            y_copy(h, lax.rem(col + d, cols)).wait_recv()
        pltpu.make_async_copy(
            stage.at[h, col], w_all[h].at[row * cols + col], ycopy.at[h]
        ).wait()
        for d in range(1, rows):
            w_copy(h, row, lax.rem(row + d, rows)).start()

    def await_w(h):
        for d in range(1, rows):
            r = lax.rem(row + d, rows)
            w_copy(h, r, r).wait_recv()

    def l_copy(p, o, way, own):
        place = l_all[p].at[pl.ds(o * cap, cap)]
        to = (col - 2, col + 2, col + 1 - 2 * core)[way]
        return pltpu.make_async_remote_copy(
            src_ref=own_l.at[p] if own else place,
            dst_ref=place,
            send_sem=lsend.at[p, o, way],
            recv_sem=lrecv.at[p, o],
            device_id=(row, to),
            device_id_type=MESH,
        )

    def l_own(p):
        return pltpu.make_async_copy(
            own_l.at[p], l_all[p].at[pl.ds(col * cap, cap)], lcopy.at[p]
        )

    leftmost = z < chips // 2
    at_end = (z == 0) | (z == chips - 1)

    def send_own(p):
        @pl.when(z > 0)
        def _():
            l_copy(p, col, 0, True).start()

        @pl.when(z < chips - 1)
        def _():
            l_copy(p, col, 1, True).start()

        l_copy(p, col, 2, True).start()
        l_own(p).start()

    def relay_left(p, d):
        left = col - 2 * d

        @pl.when(z >= d)
        def _():
            l_copy(p, left, 1, False).wait_recv()

            @pl.when(z < chips - 1)
            def _():
                l_copy(p, left, 1, False).start()

            l_copy(p, left, 2, False).start()

    def relay_right(p, d):
        right = col + 2 * d

        @pl.when(z + d < chips)
        def _():
            l_copy(p, right, 0, False).wait_recv()

            @pl.when(z > 0)
            def _():
                l_copy(p, right, 0, False).start()

            l_copy(p, right, 2, False).start()

    def relay(p):
        @pl.when(leftmost)
        def _():
            for d in range(1, chips):
                relay_right(p, d)
                relay_left(p, d)

        @pl.when(jnp.logical_not(leftmost))
        def _():
            for d in range(1, chips):
                relay_left(p, d)
                relay_right(p, d)

    def await_l(p):
        l_own(p).wait()
        for chip in range(chips):
            l_copy(p, 2 * chip + 1 - core, 2, False).wait_recv()

    def l_drain(p):
        @pl.when(z > 0)
        def _():
            l_copy(p, col, 0, True).wait_send()

        @pl.when(z < chips - 1)
        def _():
            l_copy(p, col, 1, True).wait_send()

        l_copy(p, col, 2, True).wait_send()
        for d in range(1, chips):
            left = col - 2 * d
            right = col + 2 * d

            @pl.when(z >= d)
            def _():
                @pl.when(z < chips - 1)
                def _():
                    l_copy(p, left, 1, False).wait_send()

                l_copy(p, left, 2, False).wait_send()

            @pl.when(z + d < chips)
            def _():
                @pl.when(z > 0)
                def _():
                    l_copy(p, right, 0, False).wait_send()

                l_copy(p, right, 2, False).wait_send()

    def set_real_form(at, pair):
        rf[at, :PANEL, :PANEL] = pair[0]
        rf[at, :PANEL, PANEL:] = pair[1]
        rf[at, PANEL:, :PANEL] = -pair[1]
        rf[at, PANEL:, PANEL:] = pair[0]

    send_y(0)

    fetch[1].wait()
    fetch[2].wait()
    set_real_form(0, inv1)
    coupling = jnp.dot(
        jnp.concatenate([cl[0], cl[1]], axis=1), rf[0], preferred_element_type=F32
    ).astype(BF16)
    gt[:PANEL, :PANEL] = coupling[:, :PANEL]
    gt[:PANEL, PANEL:] = -coupling[:, PANEL:]
    gt[PANEL:, :PANEL] = coupling[:, PANEL:]
    gt[PANEL:, PANEL:] = coupling[:, :PANEL]

    def low_w(i, carry):
        block = y_ref[pl.ds(i * tile, tile)].reshape(tile * BS, 4 * PANEL)
        low = half(block, 1).astype(F32) - dot_t(half(block, 0), gt[...])
        w_low[pl.ds(i * tile, tile)] = low.astype(BF16).reshape(tile, BS, 2 * PANEL)
        return carry

    lax.fori_loop(0, n_tiles, low_w, 0)
    for c in range(cols):
        stage[1, c] = w_low[slots[c]]
    send_y(1)

    def put_l(i, first, value):
        for k in range(2):
            part = jnp.concatenate(
                [
                    value[:, k * CH : (k + 1) * CH],
                    value[:, PANEL + k * CH : PANEL + (k + 1) * CH],
                ],
                axis=1,
            )
            own_l[first + k, pl.ds(i * tile, tile)] = part.reshape(tile, BS, 2 * CH)

    def first_l(i, carry):
        block = x_ref[pl.ds(i * tile, tile)].reshape(tile * BS, 4 * PANEL)
        value = jnp.dot(half(block, 0), rf[0], preferred_element_type=F32).astype(BF16)
        put_l(i, 0, value)
        return carry

    fetch[3].wait()
    lax.fori_loop(0, n_tiles, first_l, 0)
    send_own(0)
    fetch[4].wait()
    fetch[5].wait()

    set_real_form(1, cr)
    set_real_form(2, inv2)

    def second_l(i, carry):
        block = x_ref[pl.ds(i * tile, tile)].reshape(tile * BS, 4 * PANEL)
        parts = [
            own_l[k, pl.ds(i * tile, tile)].reshape(tile * BS, 2 * CH) for k in range(2)
        ]
        low = jnp.concatenate(
            [parts[0][:, :CH], parts[1][:, :CH], parts[0][:, CH:], parts[1][:, CH:]], axis=1
        )
        rest = half(block, 1).astype(F32) - jnp.dot(low, rf[1], preferred_element_type=F32)
        value = jnp.dot(rest.astype(BF16), rf[2], preferred_element_type=F32).astype(BF16)
        put_l(i, 2, value)
        return carry

    lax.fori_loop(0, n_tiles, second_l, 0)

    def update(p):
        h = p // 2

        def column(q, carry):
            group = q // PER
            owner = owner_ref[(group * cols + col) * PER + q % PER]
            rhs = w_part(w_all[h][group * cols + owner], p)
            lhs = jnp.concatenate(
                [l_all[p][place_ref[picks_ref[s, q]]] for s in range(fill)], axis=0
            )
            change = dot_t(lhs, rhs)
            lanes = pl.ds(pl.multiple_of(q * 2 * BS, 2 * BS), 2 * BS)
            if p == 0:
                acc[q] = trail_v[:, lanes].astype(F32) - change
            elif p < PARTS - 1:
                acc[q] = acc[q] - change
            else:
                out_ref[:, lanes] = (acc[q] - change).astype(BF16)
            return carry

        lax.fori_loop(0, width, column, 0)

    def finish(p):
        await_l(p)
        if p % 2 == 0:
            await_w(p // 2)
        if fused:
            if p == 0:
                trail_copy.wait()
            update(p)

    @pl.when(at_end)
    def _():
        for p in range(1, PARTS):
            send_own(p)

    spread_w(0)
    relay(0)
    spread_w(1)
    for p in range(1, PARTS):

        @pl.when(jnp.logical_not(at_end))
        def _():
            send_own(p)
            if p > 1:
                finish(p - 2)

        @pl.when(at_end)
        def _():
            finish(p - 1)

        relay(p)

    @pl.when(jnp.logical_not(at_end))
    def _():
        finish(PARTS - 2)

    finish(PARTS - 1)

    for h in range(2):
        for d in range(1, cols):
            y_copy(h, lax.rem(col + d, cols)).wait_send()
        for d in range(1, rows):
            w_copy(h, row, lax.rem(row + d, rows)).wait_send()
    for p in range(PARTS):
        l_drain(p)


def pick_body(lidx_ref, widx_ref, *refs):
    l_refs, w_refs = refs[:PARTS], refs[PARTS : PARTS + 2]
    trail_ref, out_ref = refs[PARTS + 2 :]
    total = trail_ref[...].astype(F32)
    for p in range(PARTS):
        total = total - dot_t(l_refs[p][0], w_part(w_refs[p // 2][0], p))
    out_ref[...] = total.astype(BF16)


def plan(owner_of, rows, cols, cap):
    count = PER * cols
    owners = lax.dynamic_slice_in_dim(owner_of, lax.axis_index("row") * count, count)
    at = jnp.arange(count, dtype=jnp.int32)
    same = (owners[:, None] == owners[None, :]) & (at[None, :] < at[:, None])
    return owners * cap + jnp.sum(same.astype(jnp.int32), axis=1, dtype=jnp.int32)


def pick_indices(place, trail_rows, owner_of, rows, cols):
    at = jnp.arange(place.shape[0], dtype=jnp.int32)
    lidx = jnp.sum(
        jnp.where(trail_rows[:, :, None] == at, place, 0), axis=2, dtype=jnp.int32
    )
    wanted = lax.dynamic_index_in_dim(
        owner_of.reshape(rows, cols, PER), lax.axis_index("col"), 1, keepdims=False
    )
    widx = wanted + cols * jnp.arange(rows, dtype=jnp.int32)[:, None]
    return lidx.reshape(-1), widx.reshape(-1)


def local(mesh, trail, trail_rows, owner_x, owner_y, owner_of, inv1, inv2, cr, cl):
    rows, cols = mesh.shape["row"], mesh.shape["col"]
    cap = owner_x.shape[0] // BS
    fill = trail.shape[0] // BS
    width = trail.shape[1] // (2 * BS)
    l_shape = (cols * cap, BS, 2 * CH)
    w_shape = (rows * cols, BS, 2 * PANEL)
    fused = cols * cap * BS * 4 * PANEL * 2 <= 16 << 20
    place = plan(owner_of, rows, cols, cap)
    blocks = (cap, BS, 4 * PANEL)
    fetched = [owner_y.reshape(blocks), cl, inv1, owner_x.reshape(blocks), cr, inv2]
    operands = [place, owner_of, trail_rows] + fetched
    smem = pl.BlockSpec(memory_space=pltpu.SMEM)
    vmem = pl.BlockSpec(memory_space=pltpu.VMEM)
    anywhere = pl.BlockSpec(memory_space=pl.ANY)
    hbm = pl.BlockSpec(memory_space=pltpu.HBM)
    in_specs = [smem] * 3 + [hbm] * len(fetched)
    scratch = [
        pltpu.VMEM((PARTS, cap, BS, 2 * CH), BF16),
        pltpu.VMEM((2, cols, BS, 2 * PANEL), BF16),
        pltpu.VMEM((cap, BS, 2 * PANEL), BF16),
        pltpu.VMEM((3, 2 * PANEL, 2 * PANEL), BF16),
        pltpu.VMEM((2 * PANEL, 2 * PANEL), BF16),
        *[pltpu.VMEM(array.shape, BF16) for array in fetched],
        pltpu.SemaphoreType.DMA((len(fetched),)),
        pltpu.SemaphoreType.DMA((2, cols)),
        pltpu.SemaphoreType.DMA((2, cols)),
        pltpu.SemaphoreType.DMA((2, rows)),
        pltpu.SemaphoreType.DMA((2, rows)),
        pltpu.SemaphoreType.DMA((PARTS, cols, 3)),
        pltpu.SemaphoreType.DMA((PARTS, cols)),
        pltpu.SemaphoreType.DMA((PARTS,)),
        pltpu.SemaphoreType.DMA((2,)),
    ]
    if fused:
        operands.append(trail)
        in_specs.append(hbm)
        out_shape = jax.ShapeDtypeStruct(trail.shape, BF16)
        out_specs = vmem
        scratch = [pltpu.VMEM(l_shape, BF16)] * PARTS + [pltpu.VMEM(w_shape, BF16)] * 2 + [
            pltpu.VMEM((width, fill * BS, 2 * BS), F32),
            pltpu.VMEM(trail.shape, BF16),
            pltpu.SemaphoreType.DMA,
        ] + scratch
    else:
        out_shape = [jax.ShapeDtypeStruct(l_shape, BF16)] * PARTS
        out_shape += [jax.ShapeDtypeStruct(w_shape, BF16)] * 2
        out_specs = [anywhere] * (PARTS + 2)
    result = pl.pallas_call(
        functools.partial(body, (rows, cols, cap, fill, width, fused)),
        out_shape=out_shape,
        in_specs=in_specs,
        out_specs=out_specs,
        scratch_shapes=scratch,
        compiler_params=pltpu.CompilerParams(
            collective_id=0, has_side_effects=True, vmem_limit_bytes=60 << 20
        ),
    )(*operands)
    if fused:
        return result
    lidx, widx = pick_indices(place, trail_rows, owner_of, rows, cols)
    return pl.pallas_call(
        pick_body,
        out_shape=jax.ShapeDtypeStruct(trail.shape, BF16),
        grid_spec=pltpu.PrefetchScalarGridSpec(
            num_scalar_prefetch=2,
            grid=(width, fill),
            in_specs=[
                pl.BlockSpec((1, BS, 2 * CH), lambda q, s, li, wi: (li[s * width + q], 0, 0))
            ]
            * PARTS
            + [pl.BlockSpec((1, BS, 2 * PANEL), lambda q, s, li, wi: (wi[q], 0, 0))] * 2
            + [pl.BlockSpec((BS, 2 * BS), lambda q, s, li, wi: (s, q))],
            out_specs=pl.BlockSpec((BS, 2 * BS), lambda q, s, li, wi: (s, q)),
        ),
    )(lidx, widx, *result, trail)


def solution(mesh):
    both = P(("row", "col"), None)
    placed = (P("row", "col"), P("row", "col"), both, both, P(), P(), P(), P(), P())
    return jax.shard_map(
        functools.partial(local, mesh),
        mesh=mesh,
        in_specs=placed,
        out_specs=P("row", "col"),
        check_vma=False,
    )
```

```python
import functools

import jax
import jax.numpy as jnp
from jax import lax
from jax.experimental import pallas as pl
from jax.experimental.pallas import tpu as pltpu
from jax.sharding import PartitionSpec as P

BS = 64
PANEL = 256
PER = 6
PARTS = 4
CH = 2 * PANEL // PARTS
MESH = pl.DeviceIdType.MESH
F32 = jnp.float32
BF16 = jnp.bfloat16


def dot_t(a, b):
    return lax.dot_general(a, b, (((1,), (1,)), ((), ())), preferred_element_type=F32)


def half(block, at):
    lo = at * PANEL
    return jnp.concatenate(
        [block[:, lo : lo + PANEL], block[:, 2 * PANEL + lo : 3 * PANEL + lo]], axis=1
    )


def stacked(w_real, w_imag):
    return jnp.concatenate(
        [
            jnp.concatenate([w_real, -w_imag], axis=1),
            jnp.concatenate([w_imag, w_real], axis=1),
        ],
        axis=0,
    )


def w_part(w_half, p):
    at = (p % 2) * CH
    return stacked(w_half[:, at : at + CH], w_half[:, PANEL + at : PANEL + at + CH])


def body(sizes, *refs):
    rows, cols, cap, fill, width, fused = sizes
    owner_ref, picks_ref = refs[:2]
    sources = refs[2:8]
    refs = refs[8:]
    if fused:
        trail_ref, out_ref = refs[:2]
        refs = refs[2:]
    l_all, w_all = refs[:PARTS], refs[PARTS : PARTS + 2]
    refs = refs[PARTS + 2 :]
    if fused:
        acc, trail_v, trail_sem = refs[:3]
        refs = refs[3:]
    own_l, stage, w_low, rf, gt = refs[:5]
    held = refs[5:11]
    y_ref, cl, inv1, x_ref, cr, inv2 = held
    place_ref, fetched, ysend, yrecv, wsend, wrecv, lsend, lrecv, lcopy, ycopy = refs[11:]
    row = lax.axis_index("row")
    col = lax.axis_index("col")
    chips = cols // 2
    z = col // 2
    core = col % 2
    tile = 4
    n_tiles = cap // tile

    fetch = [
        pltpu.make_async_copy(sources[i], held[i], fetched.at[i]) for i in range(len(held))
    ]
    for copy in fetch:
        copy.start()
    if fused:
        trail_copy = pltpu.make_async_copy(trail_ref, trail_v, trail_sem)
        trail_copy.start()

    barrier = pltpu.get_barrier_semaphore()
    for d in range(1, cols):
        pl.semaphore_signal(
            barrier, inc=1, device_id=(row, lax.rem(col + d, cols)), device_id_type=MESH
        )
    for d in range(1, rows):
        pl.semaphore_signal(
            barrier, inc=1, device_id=(lax.rem(row + d, rows), col), device_id_type=MESH
        )

    slots = []
    met = jnp.int32(0)
    for c in range(cols):
        slot = jnp.int32(0)
        for k in range(c * PER, (c + 1) * PER):
            mine = owner_ref[row * (PER * cols) + k] == col
            slot = jnp.where(mine, met, slot)
            met = met + jnp.where(mine, 1, 0)
        slots.append(jnp.minimum(slot, cap - 1))

    fetch[0].wait()
    for c in range(cols):
        stage[0, c] = half(y_ref[slots[c]], 0)

    pl.semaphore_wait(barrier, cols + rows - 2)

    def send_y(h):
        for d in range(1, cols):
            to = lax.rem(col + d, cols)
            pltpu.make_async_remote_copy(
                src_ref=stage.at[h, to],
                dst_ref=w_all[h].at[row * cols + col],
                send_sem=ysend.at[h, to],
                recv_sem=yrecv.at[h, col],
                device_id=(row, to),
                device_id_type=MESH,
            ).start()
        pltpu.make_async_copy(
            stage.at[h, col], w_all[h].at[row * cols + col], ycopy.at[h]
        ).start()

    def y_copy(h, o):
        return pltpu.make_async_remote_copy(
            src_ref=stage.at[h, o],
            dst_ref=w_all[h].at[row * cols + o],
            send_sem=ysend.at[h, o],
            recv_sem=yrecv.at[h, o],
            device_id=(row, o),
            device_id_type=MESH,
        )

    def w_copy(h, r, to):
        return pltpu.make_async_remote_copy(
            src_ref=w_all[h].at[pl.ds(r * cols, cols)],
            dst_ref=w_all[h].at[pl.ds(r * cols, cols)],
            send_sem=wsend.at[h, to],
            recv_sem=wrecv.at[h, r],
            device_id=(to, col),
            device_id_type=MESH,
        )

    def spread_w(h):
        for d in range(1, cols):
            y_copy(h, lax.rem(col + d, cols)).wait_recv()
        pltpu.make_async_copy(
            stage.at[h, col], w_all[h].at[row * cols + col], ycopy.at[h]
        ).wait()
        for d in range(1, rows):
            w_copy(h, row, lax.rem(row + d, rows)).start()

    def await_w(h):
        for d in range(1, rows):
            r = lax.rem(row + d, rows)
            w_copy(h, r, r).wait_recv()

    def l_copy(p, o, way, own):
        place = l_all[p].at[pl.ds(o * cap, cap)]
        to = (col - 2, col + 2, col + 1 - 2 * core)[way]
        return pltpu.make_async_remote_copy(
            src_ref=own_l.at[p] if own else place,
            dst_ref=place,
            send_sem=lsend.at[p, o, way],
            recv_sem=lrecv.at[p, o],
            device_id=(row, to),
            device_id_type=MESH,
        )

    def l_own(p):
        return pltpu.make_async_copy(
            own_l.at[p], l_all[p].at[pl.ds(col * cap, cap)], lcopy.at[p]
        )

    leftmost = z < chips // 2
    at_end = (z == 0) | (z == chips - 1)

    def send_own(p):
        @pl.when(z > 0)
        def _():
            l_copy(p, col, 0, True).start()

        @pl.when(z < chips - 1)
        def _():
            l_copy(p, col, 1, True).start()

        l_copy(p, col, 2, True).start()
        l_own(p).start()

    def relay_left(p, d):
        left = col - 2 * d

        @pl.when(z >= d)
        def _():
            l_copy(p, left, 1, False).wait_recv()

            @pl.when(z < chips - 1)
            def _():
                l_copy(p, left, 1, False).start()

            l_copy(p, left, 2, False).start()

    def relay_right(p, d):
        right = col + 2 * d

        @pl.when(z + d < chips)
        def _():
            l_copy(p, right, 0, False).wait_recv()

            @pl.when(z > 0)
            def _():
                l_copy(p, right, 0, False).start()

            l_copy(p, right, 2, False).start()

    def relay(p):
        @pl.when(leftmost)
        def _():
            for d in range(1, chips):
                relay_right(p, d)
                relay_left(p, d)

        @pl.when(jnp.logical_not(leftmost))
        def _():
            for d in range(1, chips):
                relay_left(p, d)
                relay_right(p, d)

    def await_l(p):
        l_own(p).wait()
        for chip in range(chips):
            l_copy(p, 2 * chip + 1 - core, 2, False).wait_recv()

    def l_drain(p):
        @pl.when(z > 0)
        def _():
            l_copy(p, col, 0, True).wait_send()

        @pl.when(z < chips - 1)
        def _():
            l_copy(p, col, 1, True).wait_send()

        l_copy(p, col, 2, True).wait_send()
        for d in range(1, chips):
            left = col - 2 * d
            right = col + 2 * d

            @pl.when(z >= d)
            def _():
                @pl.when(z < chips - 1)
                def _():
                    l_copy(p, left, 1, False).wait_send()

                l_copy(p, left, 2, False).wait_send()

            @pl.when(z + d < chips)
            def _():
                @pl.when(z > 0)
                def _():
                    l_copy(p, right, 0, False).wait_send()

                l_copy(p, right, 2, False).wait_send()

    def set_real_form(at, pair):
        rf[at, :PANEL, :PANEL] = pair[0]
        rf[at, :PANEL, PANEL:] = pair[1]
        rf[at, PANEL:, :PANEL] = -pair[1]
        rf[at, PANEL:, PANEL:] = pair[0]

    send_y(0)

    fetch[1].wait()
    fetch[2].wait()
    set_real_form(0, inv1)
    coupling = jnp.dot(
        jnp.concatenate([cl[0], cl[1]], axis=1), rf[0], preferred_element_type=F32
    ).astype(BF16)
    gt[:PANEL, :PANEL] = coupling[:, :PANEL]
    gt[:PANEL, PANEL:] = -coupling[:, PANEL:]
    gt[PANEL:, :PANEL] = coupling[:, PANEL:]
    gt[PANEL:, PANEL:] = coupling[:, :PANEL]

    def low_w(i, carry):
        block = y_ref[pl.ds(i * tile, tile)].reshape(tile * BS, 4 * PANEL)
        low = half(block, 1).astype(F32) - dot_t(half(block, 0), gt[...])
        w_low[pl.ds(i * tile, tile)] = low.astype(BF16).reshape(tile, BS, 2 * PANEL)
        return carry

    lax.fori_loop(0, n_tiles, low_w, 0)
    for c in range(cols):
        stage[1, c] = w_low[slots[c]]
    send_y(1)

    def put_l(i, first, value):
        for k in range(2):
            part = jnp.concatenate(
                [
                    value[:, k * CH : (k + 1) * CH],
                    value[:, PANEL + k * CH : PANEL + (k + 1) * CH],
                ],
                axis=1,
            )
            own_l[first + k, pl.ds(i * tile, tile)] = part.reshape(tile, BS, 2 * CH)

    def first_l(i, carry):
        block = x_ref[pl.ds(i * tile, tile)].reshape(tile * BS, 4 * PANEL)
        value = jnp.dot(half(block, 0), rf[0], preferred_element_type=F32).astype(BF16)
        put_l(i, 0, value)
        return carry

    fetch[3].wait()
    lax.fori_loop(0, n_tiles, first_l, 0)
    send_own(0)
    fetch[4].wait()
    fetch[5].wait()

    set_real_form(1, cr)
    set_real_form(2, inv2)

    def second_l(i, carry):
        block = x_ref[pl.ds(i * tile, tile)].reshape(tile * BS, 4 * PANEL)
        parts = [
            own_l[k, pl.ds(i * tile, tile)].reshape(tile * BS, 2 * CH) for k in range(2)
        ]
        low = jnp.concatenate(
            [parts[0][:, :CH], parts[1][:, :CH], parts[0][:, CH:], parts[1][:, CH:]], axis=1
        )
        rest = half(block, 1).astype(F32) - jnp.dot(low, rf[1], preferred_element_type=F32)
        value = jnp.dot(rest.astype(BF16), rf[2], preferred_element_type=F32).astype(BF16)
        put_l(i, 2, value)
        return carry

    lax.fori_loop(0, n_tiles, second_l, 0)

    def update(p):
        h = p // 2

        def column(q, carry):
            group = q // PER
            owner = owner_ref[(group * cols + col) * PER + q % PER]
            rhs = w_part(w_all[h][group * cols + owner], p)
            lhs = jnp.concatenate(
                [l_all[p][place_ref[picks_ref[s, q]]] for s in range(fill)], axis=0
            )
            change = dot_t(lhs, rhs)
            lanes = pl.ds(pl.multiple_of(q * 2 * BS, 2 * BS), 2 * BS)
            if p == 0:
                acc[q] = trail_v[:, lanes].astype(F32) - change
            elif p < PARTS - 1:
                acc[q] = acc[q] - change
            else:
                out_ref[:, lanes] = (acc[q] - change).astype(BF16)
            return carry

        lax.fori_loop(0, width, column, 0, unroll=4)

    def finish(p):
        await_l(p)
        if p % 2 == 0:
            await_w(p // 2)
        if fused:
            if p == 0:
                trail_copy.wait()
            update(p)

    @pl.when(at_end)
    def _():
        for p in range(1, PARTS):
            send_own(p)

    def rank(b, counts):
        owner = owner_ref[row * (PER * cols) + b]
        slot = jnp.int32(0)
        after = []
        for c in range(cols):
            slot = jnp.where(owner == c, counts[c], slot)
            after.append(counts[c] + jnp.where(owner == c, 1, 0))
        place_ref[b] = owner * cap + jnp.minimum(slot, cap - 1)
        return tuple(after)

    lax.fori_loop(0, PER * cols, rank, (jnp.int32(0),) * cols)

    spread_w(0)
    relay(0)
    spread_w(1)
    for p in range(1, PARTS):

        @pl.when(jnp.logical_not(at_end))
        def _():
            send_own(p)
            if p > 1:
                finish(p - 2)

        @pl.when(at_end)
        def _():
            finish(p - 1)

        relay(p)

    @pl.when(jnp.logical_not(at_end))
    def _():
        finish(PARTS - 2)

    finish(PARTS - 1)

    for h in range(2):
        for d in range(1, cols):
            y_copy(h, lax.rem(col + d, cols)).wait_send()
        for d in range(1, rows):
            w_copy(h, row, lax.rem(row + d, rows)).wait_send()
    for p in range(PARTS):
        l_drain(p)


def pick_body(lidx_ref, widx_ref, *refs):
    l_refs, w_refs = refs[:PARTS], refs[PARTS : PARTS + 2]
    trail_ref, out_ref = refs[PARTS + 2 :]
    total = trail_ref[...].astype(F32)
    for p in range(PARTS):
        total = total - dot_t(l_refs[p][0], w_part(w_refs[p // 2][0], p))
    out_ref[...] = total.astype(BF16)


def plan(owner_of, rows, cols, cap):
    count = PER * cols
    owners = lax.dynamic_slice_in_dim(owner_of, lax.axis_index("row") * count, count)
    at = jnp.arange(count, dtype=jnp.int32)
    same = (owners[:, None] == owners[None, :]) & (at[None, :] < at[:, None])
    return owners * cap + jnp.sum(same.astype(jnp.int32), axis=1, dtype=jnp.int32)


def pick_indices(place, trail_rows, owner_of, rows, cols):
    at = jnp.arange(place.shape[0], dtype=jnp.int32)
    lidx = jnp.sum(
        jnp.where(trail_rows[:, :, None] == at, place, 0), axis=2, dtype=jnp.int32
    )
    wanted = lax.dynamic_index_in_dim(
        owner_of.reshape(rows, cols, PER), lax.axis_index("col"), 1, keepdims=False
    )
    widx = wanted + cols * jnp.arange(rows, dtype=jnp.int32)[:, None]
    return lidx.reshape(-1), widx.reshape(-1)


def local(mesh, trail, trail_rows, owner_x, owner_y, owner_of, inv1, inv2, cr, cl):
    rows, cols = mesh.shape["row"], mesh.shape["col"]
    cap = owner_x.shape[0] // BS
    fill = trail.shape[0] // BS
    width = trail.shape[1] // (2 * BS)
    l_shape = (cols * cap, BS, 2 * CH)
    w_shape = (rows * cols, BS, 2 * PANEL)
    fused = cols * cap * BS * 4 * PANEL * 2 <= 16 << 20
    blocks = (cap, BS, 4 * PANEL)
    fetched = [owner_y.reshape(blocks), cl, inv1, owner_x.reshape(blocks), cr, inv2]
    operands = [owner_of, trail_rows] + fetched
    smem = pl.BlockSpec(memory_space=pltpu.SMEM)
    vmem = pl.BlockSpec(memory_space=pltpu.VMEM)
    anywhere = pl.BlockSpec(memory_space=pl.ANY)
    hbm = pl.BlockSpec(memory_space=pltpu.HBM)
    in_specs = [smem] * 2 + [hbm] * len(fetched)
    scratch = [
        pltpu.VMEM((PARTS, cap, BS, 2 * CH), BF16),
        pltpu.VMEM((2, cols, BS, 2 * PANEL), BF16),
        pltpu.VMEM((cap, BS, 2 * PANEL), BF16),
        pltpu.VMEM((3, 2 * PANEL, 2 * PANEL), BF16),
        pltpu.VMEM((2 * PANEL, 2 * PANEL), BF16),
        *[pltpu.VMEM(array.shape, BF16) for array in fetched],
        pltpu.SMEM((PER * cols,), jnp.int32),
        pltpu.SemaphoreType.DMA((len(fetched),)),
        pltpu.SemaphoreType.DMA((2, cols)),
        pltpu.SemaphoreType.DMA((2, cols)),
        pltpu.SemaphoreType.DMA((2, rows)),
        pltpu.SemaphoreType.DMA((2, rows)),
        pltpu.SemaphoreType.DMA((PARTS, cols, 3)),
        pltpu.SemaphoreType.DMA((PARTS, cols)),
        pltpu.SemaphoreType.DMA((PARTS,)),
        pltpu.SemaphoreType.DMA((2,)),
    ]
    if fused:
        operands.append(trail)
        in_specs.append(hbm)
        out_shape = jax.ShapeDtypeStruct(trail.shape, BF16)
        out_specs = vmem
        scratch = [pltpu.VMEM(l_shape, BF16)] * PARTS + [pltpu.VMEM(w_shape, BF16)] * 2 + [
            pltpu.VMEM((width, fill * BS, 2 * BS), F32),
            pltpu.VMEM(trail.shape, BF16),
            pltpu.SemaphoreType.DMA,
        ] + scratch
    else:
        out_shape = [jax.ShapeDtypeStruct(l_shape, BF16)] * PARTS
        out_shape += [jax.ShapeDtypeStruct(w_shape, BF16)] * 2
        out_specs = [anywhere] * (PARTS + 2)
    result = pl.pallas_call(
        functools.partial(body, (rows, cols, cap, fill, width, fused)),
        out_shape=out_shape,
        in_specs=in_specs,
        out_specs=out_specs,
        scratch_shapes=scratch,
        compiler_params=pltpu.CompilerParams(
            collective_id=0, has_side_effects=True, vmem_limit_bytes=60 << 20
        ),
    )(*operands)
    if fused:
        return result
    place = plan(owner_of, rows, cols, cap)
    lidx, widx = pick_indices(place, trail_rows, owner_of, rows, cols)
    return pl.pallas_call(
        pick_body,
        out_shape=jax.ShapeDtypeStruct(trail.shape, BF16),
        grid_spec=pltpu.PrefetchScalarGridSpec(
            num_scalar_prefetch=2,
            grid=(width, fill),
            in_specs=[
                pl.BlockSpec((1, BS, 2 * CH), lambda q, s, li, wi: (li[s * width + q], 0, 0))
            ]
            * PARTS
            + [pl.BlockSpec((1, BS, 2 * PANEL), lambda q, s, li, wi: (wi[q], 0, 0))] * 2
            + [pl.BlockSpec((BS, 2 * BS), lambda q, s, li, wi: (s, q))],
            out_specs=pl.BlockSpec((BS, 2 * BS), lambda q, s, li, wi: (s, q)),
        ),
    )(lidx, widx, *result, trail)


def solution(mesh):
    both = P(("row", "col"), None)
    placed = (P("row", "col"), P("row", "col"), both, both, P(), P(), P(), P(), P())
    return jax.shard_map(
        functools.partial(local, mesh),
        mesh=mesh,
        in_specs=placed,
        out_specs=P("row", "col"),
        check_vma=False,
    )
```

```python
import functools

import jax
import jax.numpy as jnp
from jax import lax
from jax.experimental import pallas as pl
from jax.experimental.pallas import tpu as pltpu
from jax.sharding import PartitionSpec as P

BS = 64
PANEL = 256
PER = 6
PARTS = 4
CH = 2 * PANEL // PARTS
MESH = pl.DeviceIdType.MESH
F32 = jnp.float32
BF16 = jnp.bfloat16


def dot_t(a, b):
    return lax.dot_general(a, b, (((1,), (1,)), ((), ())), preferred_element_type=F32)


def half(block, at):
    lo = at * PANEL
    return jnp.concatenate(
        [block[:, lo : lo + PANEL], block[:, 2 * PANEL + lo : 3 * PANEL + lo]], axis=1
    )


def stacked(w_real, w_imag):
    return jnp.concatenate(
        [
            jnp.concatenate([w_real, -w_imag], axis=1),
            jnp.concatenate([w_imag, w_real], axis=1),
        ],
        axis=0,
    )


def w_part(w_half, p):
    at = (p % 2) * CH
    return stacked(w_half[:, at : at + CH], w_half[:, PANEL + at : PANEL + at + CH])


def body(sizes, *refs):
    rows, cols, cap, fill, width, fused = sizes
    owner_ref, picks_ref = refs[:2]
    sources = refs[2:8]
    refs = refs[8:]
    if fused:
        trail_ref, out_ref = refs[:2]
        refs = refs[2:]
    l_all, w_all = refs[:PARTS], refs[PARTS : PARTS + 2]
    refs = refs[PARTS + 2 :]
    if fused:
        acc, trail_v, trail_sem, out_v, out_sem = refs[:5]
        refs = refs[5:]
    own_l, stage, w_low, rf, gt = refs[:5]
    held = refs[5:11]
    y_ref, cl, inv1, x_ref, cr, inv2 = held
    place_ref, fetched, ysend, yrecv, wsend, wrecv, lsend, lrecv, lcopy, ycopy = refs[11:]
    row = lax.axis_index("row")
    col = lax.axis_index("col")
    chips = cols // 2
    z = col // 2
    core = col % 2
    tile = 4
    n_tiles = cap // tile

    fetch = [
        pltpu.make_async_copy(sources[i], held[i], fetched.at[i]) for i in range(len(held))
    ]
    for copy in fetch:
        copy.start()
    if fused:
        trail_copy = pltpu.make_async_copy(trail_ref, trail_v, trail_sem)
        trail_copy.start()

    barrier = pltpu.get_barrier_semaphore()
    for d in range(1, cols):
        pl.semaphore_signal(
            barrier, inc=1, device_id=(row, lax.rem(col + d, cols)), device_id_type=MESH
        )
    for d in range(1, rows):
        pl.semaphore_signal(
            barrier, inc=1, device_id=(lax.rem(row + d, rows), col), device_id_type=MESH
        )

    slots = []
    met = jnp.int32(0)
    for c in range(cols):
        slot = jnp.int32(0)
        for k in range(c * PER, (c + 1) * PER):
            mine = owner_ref[row * (PER * cols) + k] == col
            slot = jnp.where(mine, met, slot)
            met = met + jnp.where(mine, 1, 0)
        slots.append(jnp.minimum(slot, cap - 1))

    fetch[0].wait()
    for c in range(cols):
        stage[0, c] = half(y_ref[slots[c]], 0)

    pl.semaphore_wait(barrier, cols + rows - 2)

    def send_y(h):
        for d in range(1, cols):
            to = lax.rem(col + d, cols)
            pltpu.make_async_remote_copy(
                src_ref=stage.at[h, to],
                dst_ref=w_all[h].at[row * cols + col],
                send_sem=ysend.at[h, to],
                recv_sem=yrecv.at[h, col],
                device_id=(row, to),
                device_id_type=MESH,
            ).start()
        pltpu.make_async_copy(
            stage.at[h, col], w_all[h].at[row * cols + col], ycopy.at[h]
        ).start()

    def y_copy(h, o):
        return pltpu.make_async_remote_copy(
            src_ref=stage.at[h, o],
            dst_ref=w_all[h].at[row * cols + o],
            send_sem=ysend.at[h, o],
            recv_sem=yrecv.at[h, o],
            device_id=(row, o),
            device_id_type=MESH,
        )

    def w_copy(h, r, to):
        return pltpu.make_async_remote_copy(
            src_ref=w_all[h].at[pl.ds(r * cols, cols)],
            dst_ref=w_all[h].at[pl.ds(r * cols, cols)],
            send_sem=wsend.at[h, to],
            recv_sem=wrecv.at[h, r],
            device_id=(to, col),
            device_id_type=MESH,
        )

    def spread_w(h):
        for d in range(1, cols):
            y_copy(h, lax.rem(col + d, cols)).wait_recv()
        pltpu.make_async_copy(
            stage.at[h, col], w_all[h].at[row * cols + col], ycopy.at[h]
        ).wait()
        for d in range(1, rows):
            w_copy(h, row, lax.rem(row + d, rows)).start()

    def await_w(h):
        for d in range(1, rows):
            r = lax.rem(row + d, rows)
            w_copy(h, r, r).wait_recv()

    def l_copy(p, o, way, own):
        place = l_all[p].at[pl.ds(o * cap, cap)]
        to = (col - 2, col + 2, col + 1 - 2 * core)[way]
        return pltpu.make_async_remote_copy(
            src_ref=own_l.at[p] if own else place,
            dst_ref=place,
            send_sem=lsend.at[p, o, way],
            recv_sem=lrecv.at[p, o],
            device_id=(row, to),
            device_id_type=MESH,
        )

    def l_own(p):
        return pltpu.make_async_copy(
            own_l.at[p], l_all[p].at[pl.ds(col * cap, cap)], lcopy.at[p]
        )

    leftmost = z < chips // 2
    at_end = (z == 0) | (z == chips - 1)

    def send_own(p):
        @pl.when(z > 0)
        def _():
            l_copy(p, col, 0, True).start()

        @pl.when(z < chips - 1)
        def _():
            l_copy(p, col, 1, True).start()

        l_copy(p, col, 2, True).start()
        l_own(p).start()

    def relay_left(p, d):
        left = col - 2 * d

        @pl.when(z >= d)
        def _():
            l_copy(p, left, 1, False).wait_recv()

            @pl.when(z < chips - 1)
            def _():
                l_copy(p, left, 1, False).start()

            l_copy(p, left, 2, False).start()

    def relay_right(p, d):
        right = col + 2 * d

        @pl.when(z + d < chips)
        def _():
            l_copy(p, right, 0, False).wait_recv()

            @pl.when(z > 0)
            def _():
                l_copy(p, right, 0, False).start()

            l_copy(p, right, 2, False).start()

    def relay(p):
        @pl.when(leftmost)
        def _():
            for d in range(1, chips):
                relay_right(p, d)
                relay_left(p, d)

        @pl.when(jnp.logical_not(leftmost))
        def _():
            for d in range(1, chips):
                relay_left(p, d)
                relay_right(p, d)

    def await_l(p):
        l_own(p).wait()
        for chip in range(chips):
            l_copy(p, 2 * chip + 1 - core, 2, False).wait_recv()

    def l_drain(p):
        @pl.when(z > 0)
        def _():
            l_copy(p, col, 0, True).wait_send()

        @pl.when(z < chips - 1)
        def _():
            l_copy(p, col, 1, True).wait_send()

        l_copy(p, col, 2, True).wait_send()
        for d in range(1, chips):
            left = col - 2 * d
            right = col + 2 * d

            @pl.when(z >= d)
            def _():
                @pl.when(z < chips - 1)
                def _():
                    l_copy(p, left, 1, False).wait_send()

                l_copy(p, left, 2, False).wait_send()

            @pl.when(z + d < chips)
            def _():
                @pl.when(z > 0)
                def _():
                    l_copy(p, right, 0, False).wait_send()

                l_copy(p, right, 2, False).wait_send()

    def set_real_form(at, pair):
        rf[at, :PANEL, :PANEL] = pair[0]
        rf[at, :PANEL, PANEL:] = pair[1]
        rf[at, PANEL:, :PANEL] = -pair[1]
        rf[at, PANEL:, PANEL:] = pair[0]

    send_y(0)

    fetch[1].wait()
    fetch[2].wait()
    set_real_form(0, inv1)
    coupling = jnp.dot(
        jnp.concatenate([cl[0], cl[1]], axis=1), rf[0], preferred_element_type=F32
    ).astype(BF16)
    gt[:PANEL, :PANEL] = coupling[:, :PANEL]
    gt[:PANEL, PANEL:] = -coupling[:, PANEL:]
    gt[PANEL:, :PANEL] = coupling[:, PANEL:]
    gt[PANEL:, PANEL:] = coupling[:, :PANEL]

    def low_w(i, carry):
        block = y_ref[pl.ds(i * tile, tile)].reshape(tile * BS, 4 * PANEL)
        low = half(block, 1).astype(F32) - dot_t(half(block, 0), gt[...])
        w_low[pl.ds(i * tile, tile)] = low.astype(BF16).reshape(tile, BS, 2 * PANEL)
        return carry

    lax.fori_loop(0, n_tiles, low_w, 0)
    for c in range(cols):
        stage[1, c] = w_low[slots[c]]
    send_y(1)

    def put_l(i, first, value):
        for k in range(2):
            part = jnp.concatenate(
                [
                    value[:, k * CH : (k + 1) * CH],
                    value[:, PANEL + k * CH : PANEL + (k + 1) * CH],
                ],
                axis=1,
            )
            own_l[first + k, pl.ds(i * tile, tile)] = part.reshape(tile, BS, 2 * CH)

    def first_l(i, carry):
        block = x_ref[pl.ds(i * tile, tile)].reshape(tile * BS, 4 * PANEL)
        value = jnp.dot(half(block, 0), rf[0], preferred_element_type=F32).astype(BF16)
        put_l(i, 0, value)
        return carry

    fetch[3].wait()
    lax.fori_loop(0, n_tiles, first_l, 0)
    send_own(0)
    fetch[4].wait()
    fetch[5].wait()

    set_real_form(1, cr)
    set_real_form(2, inv2)

    def second_l(i, carry):
        block = x_ref[pl.ds(i * tile, tile)].reshape(tile * BS, 4 * PANEL)
        parts = [
            own_l[k, pl.ds(i * tile, tile)].reshape(tile * BS, 2 * CH) for k in range(2)
        ]
        low = jnp.concatenate(
            [parts[0][:, :CH], parts[1][:, :CH], parts[0][:, CH:], parts[1][:, CH:]], axis=1
        )
        rest = half(block, 1).astype(F32) - jnp.dot(low, rf[1], preferred_element_type=F32)
        value = jnp.dot(rest.astype(BF16), rf[2], preferred_element_type=F32).astype(BF16)
        put_l(i, 2, value)
        return carry

    lax.fori_loop(0, n_tiles, second_l, 0)

    def write_out(g):
        lanes = pl.ds(g * PER * 2 * BS, PER * 2 * BS)
        return pltpu.make_async_copy(out_v.at[:, lanes], out_ref.at[:, lanes], out_sem.at[g])

    def update(p):
        h = p // 2

        def column(q, carry):
            group = q // PER
            owner = owner_ref[(group * cols + col) * PER + q % PER]
            rhs = w_part(w_all[h][group * cols + owner], p)
            lhs = jnp.concatenate(
                [l_all[p][place_ref[picks_ref[s, q]]] for s in range(fill)], axis=0
            )
            change = dot_t(lhs, rhs)
            lanes = pl.ds(pl.multiple_of(q * 2 * BS, 2 * BS), 2 * BS)
            if p == 0:
                acc[q] = trail_v[:, lanes].astype(F32) - change
            elif p < PARTS - 1:
                acc[q] = acc[q] - change
            else:
                out_v[:, lanes] = (acc[q] - change).astype(BF16)
            return carry

        if p < PARTS - 1:
            lax.fori_loop(0, width, column, 0, unroll=4)
            return
        for g in range(rows):
            lax.fori_loop(g * PER, (g + 1) * PER, column, 0, unroll=PER)
            write_out(g).start()
        for g in range(rows):
            write_out(g).wait()

    def finish(p):
        await_l(p)
        if p % 2 == 0:
            await_w(p // 2)
        if fused:
            if p == 0:
                trail_copy.wait()
            update(p)

    @pl.when(at_end)
    def _():
        for p in range(1, PARTS):
            send_own(p)

    def rank(b, counts):
        owner = owner_ref[row * (PER * cols) + b]
        slot = jnp.int32(0)
        after = []
        for c in range(cols):
            slot = jnp.where(owner == c, counts[c], slot)
            after.append(counts[c] + jnp.where(owner == c, 1, 0))
        place_ref[b] = owner * cap + jnp.minimum(slot, cap - 1)
        return tuple(after)

    lax.fori_loop(0, PER * cols, rank, (jnp.int32(0),) * cols)

    spread_w(0)
    relay(0)
    spread_w(1)
    for p in range(1, PARTS):

        @pl.when(jnp.logical_not(at_end))
        def _():
            send_own(p)
            if p > 1:
                finish(p - 2)

        @pl.when(at_end)
        def _():
            finish(p - 1)

        relay(p)

    @pl.when(jnp.logical_not(at_end))
    def _():
        finish(PARTS - 2)

    finish(PARTS - 1)

    for h in range(2):
        for d in range(1, cols):
            y_copy(h, lax.rem(col + d, cols)).wait_send()
        for d in range(1, rows):
            w_copy(h, row, lax.rem(row + d, rows)).wait_send()
    for p in range(PARTS):
        l_drain(p)


def pick_body(lidx_ref, widx_ref, *refs):
    l_refs, w_refs = refs[:PARTS], refs[PARTS : PARTS + 2]
    trail_ref, out_ref = refs[PARTS + 2 :]
    total = trail_ref[...].astype(F32)
    for p in range(PARTS):
        total = total - dot_t(l_refs[p][0], w_part(w_refs[p // 2][0], p))
    out_ref[...] = total.astype(BF16)


def plan(owner_of, rows, cols, cap):
    count = PER * cols
    owners = lax.dynamic_slice_in_dim(owner_of, lax.axis_index("row") * count, count)
    at = jnp.arange(count, dtype=jnp.int32)
    same = (owners[:, None] == owners[None, :]) & (at[None, :] < at[:, None])
    return owners * cap + jnp.sum(same.astype(jnp.int32), axis=1, dtype=jnp.int32)


def pick_indices(place, trail_rows, owner_of, rows, cols):
    at = jnp.arange(place.shape[0], dtype=jnp.int32)
    lidx = jnp.sum(
        jnp.where(trail_rows[:, :, None] == at, place, 0), axis=2, dtype=jnp.int32
    )
    wanted = lax.dynamic_index_in_dim(
        owner_of.reshape(rows, cols, PER), lax.axis_index("col"), 1, keepdims=False
    )
    widx = wanted + cols * jnp.arange(rows, dtype=jnp.int32)[:, None]
    return lidx.reshape(-1), widx.reshape(-1)


def local(mesh, trail, trail_rows, owner_x, owner_y, owner_of, inv1, inv2, cr, cl):
    rows, cols = mesh.shape["row"], mesh.shape["col"]
    cap = owner_x.shape[0] // BS
    fill = trail.shape[0] // BS
    width = trail.shape[1] // (2 * BS)
    l_shape = (cols * cap, BS, 2 * CH)
    w_shape = (rows * cols, BS, 2 * PANEL)
    fused = cols * cap * BS * 4 * PANEL * 2 <= 16 << 20
    blocks = (cap, BS, 4 * PANEL)
    fetched = [owner_y.reshape(blocks), cl, inv1, owner_x.reshape(blocks), cr, inv2]
    operands = [owner_of, trail_rows] + fetched
    smem = pl.BlockSpec(memory_space=pltpu.SMEM)
    anywhere = pl.BlockSpec(memory_space=pl.ANY)
    hbm = pl.BlockSpec(memory_space=pltpu.HBM)
    in_specs = [smem] * 2 + [hbm] * len(fetched)
    scratch = [
        pltpu.VMEM((PARTS, cap, BS, 2 * CH), BF16),
        pltpu.VMEM((2, cols, BS, 2 * PANEL), BF16),
        pltpu.VMEM((cap, BS, 2 * PANEL), BF16),
        pltpu.VMEM((3, 2 * PANEL, 2 * PANEL), BF16),
        pltpu.VMEM((2 * PANEL, 2 * PANEL), BF16),
        *[pltpu.VMEM(array.shape, BF16) for array in fetched],
        pltpu.SMEM((PER * cols,), jnp.int32),
        pltpu.SemaphoreType.DMA((len(fetched),)),
        pltpu.SemaphoreType.DMA((2, cols)),
        pltpu.SemaphoreType.DMA((2, cols)),
        pltpu.SemaphoreType.DMA((2, rows)),
        pltpu.SemaphoreType.DMA((2, rows)),
        pltpu.SemaphoreType.DMA((PARTS, cols, 3)),
        pltpu.SemaphoreType.DMA((PARTS, cols)),
        pltpu.SemaphoreType.DMA((PARTS,)),
        pltpu.SemaphoreType.DMA((2,)),
    ]
    if fused:
        operands.append(trail)
        in_specs.append(hbm)
        out_shape = jax.ShapeDtypeStruct(trail.shape, BF16)
        out_specs = hbm
        scratch = [pltpu.VMEM(l_shape, BF16)] * PARTS + [pltpu.VMEM(w_shape, BF16)] * 2 + [
            pltpu.VMEM((width, fill * BS, 2 * BS), F32),
            pltpu.VMEM(trail.shape, BF16),
            pltpu.SemaphoreType.DMA,
            pltpu.VMEM(trail.shape, BF16),
            pltpu.SemaphoreType.DMA((rows,)),
        ] + scratch
    else:
        out_shape = [jax.ShapeDtypeStruct(l_shape, BF16)] * PARTS
        out_shape += [jax.ShapeDtypeStruct(w_shape, BF16)] * 2
        out_specs = [anywhere] * (PARTS + 2)
    result = pl.pallas_call(
        functools.partial(body, (rows, cols, cap, fill, width, fused)),
        out_shape=out_shape,
        in_specs=in_specs,
        out_specs=out_specs,
        scratch_shapes=scratch,
        compiler_params=pltpu.CompilerParams(
            collective_id=0, has_side_effects=True, vmem_limit_bytes=60 << 20
        ),
    )(*operands)
    if fused:
        return result
    place = plan(owner_of, rows, cols, cap)
    lidx, widx = pick_indices(place, trail_rows, owner_of, rows, cols)
    return pl.pallas_call(
        pick_body,
        out_shape=jax.ShapeDtypeStruct(trail.shape, BF16),
        grid_spec=pltpu.PrefetchScalarGridSpec(
            num_scalar_prefetch=2,
            grid=(width, fill),
            in_specs=[
                pl.BlockSpec((1, BS, 2 * CH), lambda q, s, li, wi: (li[s * width + q], 0, 0))
            ]
            * PARTS
            + [pl.BlockSpec((1, BS, 2 * PANEL), lambda q, s, li, wi: (wi[q], 0, 0))] * 2
            + [pl.BlockSpec((BS, 2 * BS), lambda q, s, li, wi: (s, q))],
            out_specs=pl.BlockSpec((BS, 2 * BS), lambda q, s, li, wi: (s, q)),
        ),
    )(lidx, widx, *result, trail)


def solution(mesh):
    both = P(("row", "col"), None)
    placed = (P("row", "col"), P("row", "col"), both, both, P(), P(), P(), P(), P())
    return jax.shard_map(
        functools.partial(local, mesh),
        mesh=mesh,
        in_specs=placed,
        out_specs=P("row", "col"),
        check_vma=False,
    )
```
